32 devices in a mesh: subtree: 4 (over z), forest: 8 (over y, x, core).
Axes of the slice: x: 2, y: 2, z: 4, core: 2. Of those that a mesh axis runs over, the one named last changes fastest.
Arguments:
- panels: bfloat16 [4, 8, 1024, 2048], P('subtree', 'forest'), may hold values from -0.75 to 0.75
- pattern: int32 [4, 8, 8, 8], P('subtree', 'forest'), may hold values from 0 to 1, as said below
- child_map: int32 [4, 8, 8], P('subtree', 'forest'), may hold values from 0 to 7, each once within a row
- ancestor_map: int32 [4, 8, 8], P('subtree', 'forest'), may hold values from 0 to 23, as said below
Outputs:
- ancestors: float32 [4, 24, 256, 128], P('subtree', 'forest')
The draws below stay inside these ranges and needn't reach their ends.
Inputs may be any that keep to these rules, and one draw needn't show every extreme that they name: pattern[s, f, i, j] = pattern[s, f, i, i] * pattern[s, f, j, j], so each pattern is symmetric; every panel has at least one occupied and at least one empty block row. No two entries of ancestor_map[s, f, :] have the same value of entry // 3.
All inputs are finite; a program needn't handle non-finite values.
Results may differ from the reference program's by a relative error of at most 0.0003.
Values sent between devices are 32-bit elements; how exact they have to be, the bound alone decides.
No kernel may reach another device: no remote copies, remote signals or barrier semaphores. Data moves between devices by JAX's collectives and lax.ppermute only.
A program may use at most 64 MiB of HBM per device.

```python
import jax
import jax.numpy as jnp
from jax import lax

K = 2048
BLOCK = 128
NB = 8
ANC_DEV = 3
SUBS = 4
TREES = 8
R = 1024
PIECE = 256
ANC = 24


def draw_pattern(key, part):
    count = SUBS * TREES
    occupied = (jax.random.randint(jax.random.fold_in(key, 41), (count, NB), 0, 100) < 63).astype(jnp.int32)
    pick = jax.random.randint(jax.random.fold_in(key, 43), (count, 1), 0, NB)
    column = jnp.arange(NB, dtype=jnp.int32)[None, :]
    occupied = jnp.where(column == pick, 1, jnp.where(column == (pick + 1) % NB, 0, occupied)).astype(jnp.int32)
    pattern_all = occupied[:, :, None] * occupied[:, None, :]
    return pattern_all.reshape(SUBS, TREES, NB, NB).astype(jnp.int32)


def draw_ancestor_map(key, part):
    count = SUBS * TREES
    keys = jax.random.split(jax.random.fold_in(key, 17), count)
    owners = jax.vmap(lambda one_key: jax.random.permutation(one_key, TREES)[:NB])(keys)
    slots = jax.random.randint(jax.random.fold_in(key, 29), (count, NB), 0, ANC_DEV)
    first_owner = jnp.concatenate([jnp.zeros((1,), jnp.int32), jnp.arange(TREES - NB + 1, TREES, dtype=jnp.int32)])
    first_slot = jnp.concatenate([jnp.zeros((NB - 1,), jnp.int32), jnp.full((1,), ANC_DEV - 1, jnp.int32)])
    device_rank = jnp.arange(count, dtype=jnp.int32)[:, None]
    owners = jnp.where(device_rank == 0, first_owner[None, :], owners.astype(jnp.int32))
    slots = jnp.where(device_rank == 0, first_slot[None, :], slots.astype(jnp.int32))
    return (owners * ANC_DEV + slots).reshape(SUBS, TREES, NB).astype(jnp.int32)


def block_levels(key, shape, shards, smallest, high):
    def one(position, blocks):
        draws = jax.random.uniform(jax.random.fold_in(jax.random.fold_in(key, 6), position), (blocks,), jnp.float32, smallest / len(shards), high / len(shards))
        return jnp.repeat(jnp.exp(draws), shape[position] // blocks).reshape((-1,) + (1,) * (len(shape) - position - 1))

    level = one(*shards[0])
    for cut in shards[1:]:
        level = level * one(*cut)
    return level


def gaussian(own_key, dims, scale, bound, cuts=(), kind=jnp.bfloat16):
    array = jax.random.normal(own_key, dims, jnp.float32) * scale
    if len(cuts) > 0:
        array = block_levels(own_key, dims, cuts, -0.22, 0.18) * array
    return jnp.clip(array, min=-bound, max=bound).astype(kind)


def setup_inputs(seed: int = 0) -> dict:
    streams_of = jax.random.split(jax.random.key(seed), 5)
    return {
        "panels": gaussian(streams_of[0], (SUBS, TREES, R, K), 0.125, 0.75, ((0, 4), (1, 8))),
        "pattern": draw_pattern(jax.random.fold_in(streams_of[4], 71), 0),
        "child_map": jax.vmap(lambda own: jax.random.permutation(own, NB))(jax.random.split(streams_of[2], SUBS * TREES)).reshape((SUBS, TREES, NB)).astype(jnp.int32),
        "ancestor_map": draw_ancestor_map(jax.random.fold_in(streams_of[4], 71), 0),
    }


def contribution(panel_one, pattern_one, map_one):
    blocks = panel_one.reshape(NB, BLOCK, K).astype(jnp.float32)
    one_hot = (map_one[:, None] == jnp.arange(NB, dtype=jnp.int32)[None, :]).astype(jnp.float32)
    reordered = jnp.einsum("im,ipk->mpk", one_hot, blocks, precision=lax.Precision.HIGHEST).astype(jnp.bfloat16)
    flat_rows = reordered.reshape(R, K)
    moved_pattern = jnp.dot(jnp.dot(one_hot.T, pattern_one.astype(jnp.float32), precision=lax.Precision.HIGHEST), one_hot, precision=lax.Precision.HIGHEST)
    update = jnp.dot(flat_rows, flat_rows.T, preferred_element_type=jnp.float32)
    return (update.reshape(NB, BLOCK, NB, BLOCK) * moved_pattern[:, None, :, None]).reshape(R, R)


def reference(panels, pattern, child_map, ancestor_map):
    def forest_total(forest_index):
        def accumulate(running, sub_index):
            term = contribution(panels[sub_index, forest_index], pattern[sub_index, forest_index], child_map[sub_index, forest_index])
            return running + term, None
        running, unused = lax.scan(accumulate, jnp.zeros((R, R), jnp.float32), jnp.arange(SUBS, dtype=jnp.int32))
        return running

    parent = lax.map(forest_total, jnp.arange(TREES, dtype=jnp.int32))
    pieces = parent.reshape(TREES, SUBS, PIECE, NB, BLOCK).transpose(1, 0, 3, 2, 4)
    slot_hot = (ancestor_map[..., None] == jnp.arange(ANC, dtype=jnp.int32)).astype(jnp.float32)
    return jnp.einsum("sfca,sfcpq->sapq", slot_hot, pieces, precision=lax.Precision.HIGHEST)
```

```python
import functools

import jax
import jax.numpy as jnp
from jax import lax
from jax.experimental import pallas as pl
from jax.experimental.pallas import tpu as pltpu
from jax.sharding import PartitionSpec as P

ANC_DEV = 3
META = 8
CUT = 16
CHUNK_PARTS = (3, 3, 2)
VMEM_LIMIT = 44 * 1024 * 1024


def swapped(shard, axis, apart):
    return lax.ppermute(shard, axis, [(i, i ^ apart) for i in range(lax.axis_size(axis))])


def smem_spec():
    return pl.BlockSpec(memory_space=pltpu.SMEM)


def vmem_spec():
    return pl.BlockSpec(memory_space=pltpu.VMEM)


def first_empty(nb, per_piece, my_sub, child_ref, pattern_ref, inverse):
    for i in range(nb):
        inverse[child_ref[0, 0, i]] = i
    empty = jnp.int32(nb - 1)
    for place in range(nb - 1, -1, -1):
        i = inverse[position_of(place, per_piece, my_sub)]
        empty = jnp.where(pattern_ref[0, 0, i, i] == 0, jnp.int32(place), empty)
    return empty


def position_of(place, per_piece, my_sub):
    return ((place // per_piece) ^ my_sub) * per_piece + place % per_piece


def multiply_kernel(nb, per_piece, chunk_rows, child_ref, pattern_ref, panel_ref, *refs):
    out_refs = refs[: len(chunk_rows)]
    left, inverse = refs[len(chunk_rows) :]
    block = panel_ref.shape[0] // nb
    my_sub = lax.axis_index("subtree")
    empty = first_empty(nb, per_piece, my_sub, child_ref, pattern_ref, inverse)
    rows = []
    for k in range(nb - 1):
        place = k + (empty <= k).astype(jnp.int32)
        rows.append(inverse[position_of(place, per_piece, my_sub)])
    start = 0
    at = 0
    for count in chunk_rows:
        for k in range(nb - 1):
            source = pl.multiple_of(rows[k] * block + start, CUT)
            left[pl.ds(at, count), :] = panel_ref[pl.ds(source, count), :]
            at += count
        start += count
    wide = 2 * block if nb % 2 == 0 else block
    for n in range(nb * block // wide):
        product = lax.dot_general(
            left[...],
            panel_ref[pl.ds(n * wide, wide), :],
            (((1,), (1,)), ((), ())),
            preferred_element_type=jnp.float32,
        )
        at = 0
        for out_ref, count in zip(out_refs, chunk_rows):
            for k in range(nb - 1):
                for part in range(wide // block):
                    j = n * (wide // block) + part
                    scale = pattern_ref[0, 0, rows[k], j].astype(jnp.float32)
                    out_ref[k, :, pl.ds(j * block, block)] = (
                        product[at : at + count, part * block : (part + 1) * block] * scale
                    )
                at += count


def route_kernel(nb, per_piece, subs, child_ref, pattern_ref, *refs):
    slot_refs = refs[:subs]
    update_ref, same_ref, other_ref, inverse, goal = refs[subs:]
    count = update_ref.shape[1]
    block = same_ref.shape[2]
    my_sub = lax.axis_index("subtree")
    my_tree = lax.axis_index("forest")
    empty = first_empty(nb, per_piece, my_sub, child_ref, pattern_ref, inverse)
    tail = (nb - 1) * count
    same_ref[:, pl.ds(tail, META), :] = jnp.zeros((same_ref.shape[0], META, block), jnp.float32)
    other_ref[:, pl.ds(tail, META), :] = jnp.zeros((same_ref.shape[0], META, block), jnp.float32)
    mark = jnp.full((same_ref.shape[0], 1, block), empty.astype(jnp.float32), jnp.float32)
    same_ref[:, pl.ds(tail, 1), :] = mark
    other_ref[:, pl.ds(tail, 1), :] = mark
    for apart in range(subs):
        for j in range(nb):
            entry = slot_refs[apart][0, 0, child_ref[0, 0, j]]
            owner = lax.div(entry, ANC_DEV)
            to = owner ^ my_tree
            goal[apart, j] = to
            slot = (entry - owner * ANC_DEV).astype(jnp.float32)
            row = jnp.full((1, block), slot, jnp.float32)

            @pl.when(to & 1 == 0)
            def _():
                same_ref[to >> 1, pl.ds(tail + 1 + apart, 1), :] = row

            @pl.when(to & 1 == 1)
            def _():
                other_ref[to >> 1, pl.ds(tail + 1 + apart, 1), :] = row

    for k in range(nb - 1):
        place = k + (empty <= k).astype(jnp.int32)
        apart = place // per_piece
        for j in range(nb):
            to = goal[apart, j]

            @pl.when(to & 1 == 0)
            def _():
                same_ref[to >> 1, pl.ds(k * count, count), :] = update_ref[k, :, pl.ds(j * block, block)]

            @pl.when(to & 1 == 1)
            def _():
                other_ref[to >> 1, pl.ds(k * count, count), :] = update_ref[k, :, pl.ds(j * block, block)]


def gather_kernel(nb, per_piece, count, *refs):
    subs = nb // per_piece
    in_refs, out_refs = refs[:-subs], refs[-subs:]
    tail = (nb - 1) * count
    block = in_refs[0].shape[-1]
    sources = []
    for ref in in_refs:
        for index in range(ref.shape[0]):
            sources.append(ref.at[index])
    for apart in range(subs):
        for part in range(per_piece):
            place = apart * per_piece + part
            sums = [jnp.zeros((count, block), jnp.float32) for _ in range(ANC_DEV)]
            for source in sources:
                empty = source[pl.ds(tail, 1), :]
                slot = source[pl.ds(tail + 1 + apart, 1), :]
                low = source[pl.ds(min(place, nb - 2) * count, count), :]
                high = source[pl.ds(max(place - 1, 0) * count, count), :]
                value = jnp.where(empty > place, low, jnp.where(empty < place, high, 0.0))
                for index in range(ANC_DEV):
                    sums[index] += jnp.where(slot == index, value, 0.0)
            for index in range(ANC_DEV):
                out_refs[apart][index, part] = sums[index]


def finish_kernel(subs, chunk_rows, *refs):
    out_ref = refs[-1]
    start = 0
    for c, count in enumerate(chunk_rows):
        parts = refs[c * subs : (c + 1) * subs]
        total = parts[0][...]
        for part in parts[1:]:
            total += part[...]
        out_ref[0, :, :, pl.ds(start, count), :] = total
        start += count


def per_device_blocks(panels, pattern, child_map, ancestor_map):
    row_total, pivot_width = panels.shape[2:]
    nb = child_map.shape[2]
    block = row_total // nb
    subs = lax.axis_size("subtree")
    trees = lax.axis_size("forest")
    per_piece = nb // subs
    units = block // CUT
    chunk_rows = []
    for index, share in enumerate(CHUNK_PARTS):
        chunk_rows.append(units * share // sum(CHUNK_PARTS) * CUT)
    chunk_rows[-1] += block - sum(chunk_rows)
    chips = trees // 2
    params = pltpu.CompilerParams(vmem_limit_bytes=VMEM_LIMIT)

    slots = [ancestor_map] + [swapped(ancestor_map, "subtree", apart) for apart in range(1, subs)]
    updates = pl.pallas_call(
        functools.partial(multiply_kernel, nb, per_piece, chunk_rows),
        out_shape=[jax.ShapeDtypeStruct((nb - 1, count, row_total), jnp.float32) for count in chunk_rows],
        in_specs=[smem_spec(), smem_spec(), vmem_spec()],
        out_specs=[vmem_spec()] * len(chunk_rows),
        scratch_shapes=[
            pltpu.VMEM(((nb - 1) * block, pivot_width), jnp.bfloat16),
            pltpu.SMEM((nb,), jnp.int32),
        ],
        compiler_params=params,
    )(child_map, pattern, panels.reshape(row_total, pivot_width))

    pieces = []
    for count, update in zip(chunk_rows, updates):
        rows = (nb - 1) * count + META
        same, other = pl.pallas_call(
            functools.partial(route_kernel, nb, per_piece, subs),
            out_shape=[jax.ShapeDtypeStruct((chips, rows, block), jnp.float32)] * 2,
            in_specs=[smem_spec()] * (2 + subs) + [vmem_spec()],
            out_specs=[vmem_spec()] * 2,
            scratch_shapes=[pltpu.SMEM((nb,), jnp.int32), pltpu.SMEM((subs, nb), jnp.int32)],
            compiler_params=params,
        )(child_map, pattern, *slots, update)
        crossed = swapped(other, "forest", 1)
        arrived = [same[:1], crossed[:1]]
        for chip in range(1, chips):
            both = jnp.stack([same[chip], crossed[chip]])
            arrived.append(swapped(both, "forest", 2 * chip))
        piece_shape = jax.ShapeDtypeStruct((ANC_DEV, per_piece, count, block), jnp.float32)
        sums = pl.pallas_call(
            functools.partial(gather_kernel, nb, per_piece, count),
            out_shape=[piece_shape] * subs,
            in_specs=[vmem_spec()] * len(arrived),
            out_specs=[vmem_spec()] * subs,
            compiler_params=params,
        )(*arrived)
        pieces.append(sums[0])
        for apart in range(1, subs):
            pieces.append(swapped(sums[apart], "subtree", apart))
    out = pl.pallas_call(
        functools.partial(finish_kernel, subs, chunk_rows),
        out_shape=jax.ShapeDtypeStruct((1, ANC_DEV, per_piece, block, block), jnp.float32),
        in_specs=[vmem_spec()] * len(pieces),
        out_specs=vmem_spec(),
        compiler_params=params,
    )(*pieces)
    return out.reshape(1, ANC_DEV, per_piece * block, block)


def per_device_halving(panels, pattern, child_map, ancestor_map):
    row_total = panels.shape[2]
    pivot_width = panels.shape[3]
    block_count = child_map.shape[2]
    block_rows = row_total // block_count
    blocks = panels[0, 0].reshape(block_count, block_rows, pivot_width)
    one_hot = child_map[0, 0][:, None] == jnp.arange(block_count, dtype=jnp.int32)[None, :]
    reordered = jnp.einsum(
        "im,ipk->mpk", one_hot.astype(jnp.bfloat16), blocks, preferred_element_type=jnp.float32
    ).astype(jnp.bfloat16)
    flat_rows = reordered.reshape(row_total, pivot_width)
    hot_float = one_hot.astype(jnp.float32)
    moved_pattern = jnp.dot(
        jnp.dot(hot_float.T, pattern[0, 0].astype(jnp.float32), precision=lax.Precision.HIGHEST),
        hot_float,
        precision=lax.Precision.HIGHEST,
    )
    update = lax.dot_general(
        flat_rows, flat_rows, (((1,), (1,)), ((), ())), preferred_element_type=jnp.float32
    )
    update = (
        update.reshape(block_count, block_rows, block_count, block_rows)
        * moved_pattern[:, None, :, None]
    ).reshape(row_total, row_total)
    sub_count = lax.axis_size("subtree")
    depth = sub_count.bit_length() - 1
    my_index = lax.axis_index("subtree")
    holding = update
    for depth_step in range(depth):
        bit_number = depth - 1 - depth_step
        half_rows = holding.shape[0] // 2
        low_half = holding[:half_rows]
        high_half = holding[half_rows:]
        high_side = my_index >> bit_number & 1 == 1
        kept_half = jnp.where(high_side, high_half, low_half)
        sent_half = jnp.where(high_side, low_half, high_half)
        holding = kept_half + swapped(sent_half, "subtree", 1 << bit_number)
    piece_rows = holding.shape[0]
    column_blocks = holding.reshape(piece_rows, block_count, block_rows).transpose(1, 0, 2)
    slot_values = ancestor_map[0, 0]
    tree_count = lax.axis_size("forest")
    every_slot = lax.all_gather(slot_values, "forest", axis=0, tiled=True)
    owner_of = slot_values // ANC_DEV
    owner_hot = (owner_of[:, None] == jnp.arange(tree_count, dtype=jnp.int32)[None, :]).astype(
        jnp.float32
    )
    outgoing = jnp.einsum("co,cpq->opq", owner_hot, column_blocks, precision=lax.Precision.HIGHEST)
    incoming = lax.all_to_all(outgoing, "forest", split_axis=0, concat_axis=0, tiled=True)
    forest_index = lax.axis_index("forest")
    every_slot = every_slot.reshape(tree_count, block_count)
    mine_mask = every_slot // ANC_DEV == forest_index
    local_slot = every_slot % ANC_DEV
    source_hot = jnp.sum(
        jnp.where(
            mine_mask[:, :, None],
            (local_slot[:, :, None] == jnp.arange(ANC_DEV, dtype=jnp.int32)[None, None, :]).astype(
                jnp.float32
            ),
            0.0,
        ),
        axis=1,
    )
    summed = jnp.einsum("sk,spq->kpq", source_hot, incoming, precision=lax.Precision.HIGHEST)
    return summed[None]


def solution(mesh):
    in_specs = (
        P("subtree", "forest", None, None),
        P("subtree", "forest", None, None),
        P("subtree", "forest", None),
        P("subtree", "forest", None),
    )
    out_specs = P("subtree", "forest", None, None)

    def per_device(panels, pattern, child_map, ancestor_map):
        nb = child_map.shape[2]
        subs, trees = mesh.shape["subtree"], mesh.shape["forest"]
        if nb == trees and nb % subs == 0 and subs < META and trees % 2 == 0:
            return per_device_blocks(panels, pattern, child_map, ancestor_map)
        return per_device_halving(panels, pattern, child_map, ancestor_map)

    return jax.shard_map(
        per_device, mesh=mesh, in_specs=in_specs, out_specs=out_specs, check_vma=False
    )
```

```python
import functools

import jax
import jax.numpy as jnp
from jax import lax
from jax.experimental import pallas as pl
from jax.experimental.pallas import tpu as pltpu
from jax.sharding import PartitionSpec as P

ANC_DEV = 3
META = 8
CUT = 16
CHUNK_PARTS = (2, 2, 2, 2)
DEPS = ((1,), (1,), (2,))
ZWAIT = 2
ZDEP = 2
GATHER_COST = 128 * 1024 * 1024
VMEM_LIMIT = 44 * 1024 * 1024


def swapped(shard, axis, apart):
    return lax.ppermute(shard, axis, [(i, i ^ apart) for i in range(lax.axis_size(axis))])


def smem_spec():
    return pl.BlockSpec(memory_space=pltpu.SMEM)


def vmem_spec():
    return pl.BlockSpec(memory_space=pltpu.VMEM)


def place_of(position, per_piece, my_sub):
    return ((position // per_piece) ^ my_sub) * per_piece + position % per_piece


def multiply_kernel(nb, per_piece, spans, child_any, pattern_any, map_any, panel_any, *refs):
    out_refs = refs[: len(spans)]
    plan_ref, panel_ref, child_ref, pattern_ref, map_ref, sems = refs[len(spans) :]
    block = panel_any.shape[0] // nb
    small = [
        pltpu.make_async_copy(child_any, child_ref, sems.at[nb]),
        pltpu.make_async_copy(pattern_any, pattern_ref, sems.at[nb + 1]),
        pltpu.make_async_copy(map_any, map_ref, sems.at[nb + 2]),
    ]
    for copy in small:
        copy.start()
    large = []
    for i in range(nb):
        rows = pl.ds(i * block, block)
        large.append(pltpu.make_async_copy(panel_any.at[rows, :], panel_ref.at[rows, :], sems.at[i]))
        large[-1].start()
    for copy in small:
        copy.wait()
    my_sub = lax.axis_index("subtree")
    columns = [child_ref[0, 0, i] for i in range(nb)]
    places = [place_of(column, per_piece, my_sub) for column in columns]
    empty = jnp.int32(nb)
    for i in range(nb):
        empty = jnp.where((pattern_ref[0, 0, i, i] == 0) & (places[i] < empty), places[i], empty)
    kept = []
    for i in range(nb):
        kept.append(jnp.where(places[i] == empty, nb - 1, places[i] - (places[i] > empty).astype(jnp.int32)))
        plan_ref[0, i] = map_ref[0, 0, i]
        plan_ref[1, i] = empty

    def put(i, j, value):
        for out_ref, (start, count) in zip(out_refs, spans):
            out_ref[columns[j], pl.ds(pl.multiple_of(kept[i] * count, CUT), count), :] = value[start : start + count]

    for copy in large:
        copy.wait()
    for first in range(nb - 2, -1, -2):
        product = lax.dot_general(
            panel_ref[pl.ds(first * block, (nb - first) * block), :],
            panel_ref[pl.ds(first * block, 2 * block), :],
            (((1,), (1,)), ((), ())),
            preferred_element_type=jnp.float32,
        )
        for i in range(first, nb):
            for j in (first, first + 1):
                scale = pattern_ref[0, 0, i, j].astype(jnp.float32)
                value = (
                    product[(i - first) * block : (i - first + 1) * block, (j - first) * block : (j - first + 1) * block]
                    * scale
                )
                put(i, j, value)
                if i > first + 1:
                    put(j, i, value.T)


def route_kernel(nb, per_piece, subs, counts, extra, plan_ref, *refs):
    slot_refs = refs[: subs - 1]
    update_refs = refs[subs - 1 : subs - 1 + len(counts)]
    out_ref, goal = refs[subs - 1 + len(counts) + extra :]
    block = out_ref.shape[2]
    my_tree = lax.axis_index("forest")
    half = out_ref.shape[0] // 2
    empty = plan_ref[1, 0]
    tails = []
    at = 0
    for count in counts:
        tails.append(at + (nb - 1) * count)
        at = tails[-1] + META
    for tail in tails:
        out_ref[:, pl.ds(tail, META), :] = jnp.full((out_ref.shape[0], META, block), empty.astype(jnp.float32))
    for apart in range(subs):
        for c in range(nb):
            entry = plan_ref[0, c] if apart == 0 else slot_refs[apart - 1][0, 0, c]
            owner = lax.div(entry, ANC_DEV)
            to = owner ^ my_tree
            to = (to & 1) * half + (to >> 1)
            goal[apart, c] = to
            slot = (entry - owner * ANC_DEV).astype(jnp.float32)
            for tail in tails:
                out_ref[to, pl.ds(tail + 1 + apart, 1), :] = jnp.full((1, block), slot, jnp.float32)
    for k in range(nb - 1):
        place = k + (empty <= k).astype(jnp.int32)
        apart = place // per_piece
        for c in range(nb):
            to = goal[apart, c]
            for tail, count, update_ref in zip(tails, counts, update_refs):
                out_ref[to, pl.ds(tail - (nb - 1 - k) * count, count), :] = update_ref[c, pl.ds(k * count, count), :]


def gather_kernel(nb, per_piece, count, extra, *refs):
    subs = nb // per_piece
    in_refs, out_refs = refs[: len(refs) - subs - extra], refs[-subs:]
    tail = (nb - 1) * count
    block = in_refs[0].shape[-1]
    sources = []
    for ref in in_refs:
        for index in range(ref.shape[0]):
            sources.append(ref.at[index])
    for apart in range(subs):
        for part in range(per_piece):
            place = apart * per_piece + part
            sums = [jnp.zeros((count, block), jnp.float32) for _ in range(ANC_DEV)]
            for source in sources:
                empty = source[pl.ds(tail, 1), :]
                slot = source[pl.ds(tail + 1 + apart, 1), :]
                low = source[pl.ds(min(place, nb - 2) * count, count), :]
                high = source[pl.ds(max(place - 1, 0) * count, count), :]
                value = jnp.where(empty > place, low, jnp.where(empty < place, high, 0.0))
                for index in range(ANC_DEV):
                    sums[index] += jnp.where(slot == index, value, 0.0)
            for index in range(ANC_DEV):
                out_refs[apart][index, part] = sums[index]


def pack_kernel(chip, same_ref, crossed_ref, *refs):
    refs[-1][0] = same_ref[chip]
    refs[-1][1] = crossed_ref[chip]


def pack(params, chip, same, crossed, *earlier):
    return pl.pallas_call(
        functools.partial(pack_kernel, chip),
        out_shape=jax.ShapeDtypeStruct((2, *same.shape[1:]), jnp.float32),
        in_specs=[vmem_spec()] * 2 + [pl.BlockSpec(memory_space=pl.ANY)] * len(earlier),
        out_specs=vmem_spec(),
        compiler_params=params,
    )(same, crossed, *earlier)


def gather(params, nb, per_piece, count, arrived, earlier):
    subs = nb // per_piece
    block = arrived[0].shape[-1]
    return pl.pallas_call(
        functools.partial(gather_kernel, nb, per_piece, count, len(earlier)),
        out_shape=[jax.ShapeDtypeStruct((ANC_DEV, per_piece, count, block), jnp.float32)] * subs,
        in_specs=[vmem_spec()] * len(arrived) + [pl.BlockSpec(memory_space=pl.ANY)] * len(earlier),
        out_specs=[vmem_spec()] * subs,
        compiler_params=params,
        cost_estimate=pl.CostEstimate(flops=0, bytes_accessed=GATHER_COST, transcendentals=0),
    )(*arrived, *earlier)


def add_kernel(places, *refs):
    came_ref, out_refs = refs[len(places)], refs[-len(places) :]
    for held_ref, place, out_ref in zip(refs, places, out_refs):
        out_ref[...] = held_ref[...] + came_ref[place]


def send(held, apart):
    going = [index for index in held if index & apart]
    return going, swapped(jnp.stack([held[index] for index in going]), "subtree", apart)


def settle(params, held, parts, apart, going, came, earlier):
    parts.append(came[going.index(apart)])
    for index in going:
        del held[index]
    kept = [index ^ apart for index in going if index != apart]
    if kept:
        sums = pl.pallas_call(
            functools.partial(add_kernel, [going.index(index ^ apart) for index in kept]),
            out_shape=[jax.ShapeDtypeStruct(came.shape[1:], came.dtype)] * len(kept),
            in_specs=[vmem_spec()] * (len(kept) + 1) + [pl.BlockSpec(memory_space=pl.ANY)] * len(earlier),
            out_specs=[vmem_spec()] * len(kept),
            compiler_params=params,
        )(*[held[index] for index in kept], came, *earlier)
        held.update(zip(kept, sums))


def finish_kernel(chunk_rows, shares, *refs):
    out_ref = refs[-1]
    start = at = 0
    for count, share in zip(chunk_rows, shares):
        total = refs[at][...]
        for part in refs[at + 1 : at + share]:
            total += part[...]
        out_ref[0, :, :, pl.ds(start, count), :] = total
        start += count
        at += share


def per_device_blocks(panels, pattern, child_map, ancestor_map):
    row_total, pivot_width = panels.shape[2:]
    nb = child_map.shape[2]
    block = row_total // nb
    subs = lax.axis_size("subtree")
    trees = lax.axis_size("forest")
    per_piece = nb // subs
    units = block // CUT
    chunk_rows = []
    for index, share in enumerate(CHUNK_PARTS):
        chunk_rows.append(units * share // sum(CHUNK_PARTS) * CUT)
    chunk_rows[-1] += block - sum(chunk_rows)
    chips = trees // 2
    params = pltpu.CompilerParams(vmem_limit_bytes=VMEM_LIMIT)

    panel = panels.reshape(row_total, pivot_width)
    spans = []
    for count in chunk_rows:
        spans.append((sum(chunk_rows[: len(spans)]), count))
    slots = [swapped(ancestor_map, "subtree", apart) for apart in range(1, subs)]
    updates = pl.pallas_call(
        functools.partial(multiply_kernel, nb, per_piece, spans),
        out_shape=[jax.ShapeDtypeStruct((nb, nb * count, block), jnp.float32) for count in chunk_rows]
        + [jax.ShapeDtypeStruct((2, nb), jnp.int32)],
        in_specs=[pl.BlockSpec(memory_space=pltpu.HBM)] * 4,
        out_specs=[vmem_spec()] * len(spans) + [smem_spec()],
        scratch_shapes=[
            pltpu.VMEM((row_total, pivot_width), jnp.bfloat16),
            pltpu.SMEM(child_map.shape, jnp.int32),
            pltpu.SMEM(pattern.shape, jnp.int32),
            pltpu.SMEM(ancestor_map.shape, jnp.int32),
            pltpu.SemaphoreType.DMA((nb + 3,)),
        ],
        compiler_params=params,
        cost_estimate=pl.CostEstimate(
            flops=2 * nb * block * row_total * pivot_width,
            bytes_accessed=2 * row_total * pivot_width,
            transcendentals=0,
        ),
    )(*[pltpu.with_memory_space_constraint(array, pltpu.HBM) for array in (child_map, pattern, ancestor_map, panel)])
    plan = updates[-1]
    laid = []
    earlier = []
    for first, end in ((0, 1), (1, len(spans))):
        counts = chunk_rows[first:end]
        blocks = pl.pallas_call(
            functools.partial(route_kernel, nb, per_piece, subs, counts, len(earlier)),
            out_shape=jax.ShapeDtypeStruct(
                (trees, (nb - 1) * sum(counts) + META * len(counts), block), jnp.float32
            ),
            in_specs=[smem_spec()] * subs
            + [vmem_spec()] * len(counts)
            + [pl.BlockSpec(memory_space=pl.ANY)] * len(earlier),
            out_specs=vmem_spec(),
            scratch_shapes=[pltpu.SMEM((subs, nb), jnp.int32)],
            compiler_params=params,
        )(plan, *slots, *updates[first:end], *earlier)
        same, crossed = blocks[:chips], swapped(blocks[chips:], "forest", 1)
        at = 0
        for count in counts:
            rows = (nb - 1) * count + META
            laid.append((same[:, at : at + rows], crossed[:, at : at + rows]))
            at += rows
        if first == 0:
            going_out = [pack(params, chip, *laid[0]) for chip in range(1, chips)]
            earlier = going_out

    pieces = []
    arrivals = []
    open_sums = None
    for c, count in enumerate(chunk_rows):
        arrived = [laid[c][0][:1], laid[c][1][:1]]
        for chip in range(1, chips):
            arrived.append(swapped(going_out[chip - 1], "forest", 2 * chip))
        arrivals.append(arrived)
        waits = []
        if c < len(chunk_rows) - 1:
            going_out = []
            for chip in range(1, chips):
                earlier = [arrived[index + 1] for index in DEPS[chip - 1]]
                if chip == 2 and c > 1 and ZDEP:
                    earlier.append(pieces[c - 2][-1])
                going_out.append(pack(params, chip, *laid[c + 1], *earlier))
            waits = list(going_out)
        if open_sums is not None:
            held, apart = open_sums[0], 1
            settle(params, held, pieces[-1], apart, *open_sums[1:], waits[:ZWAIT])
            while 2 * apart < subs:
                apart *= 2
                settle(params, held, pieces[-1], apart, *send(held, apart), [])
        sums = gather(params, nb, per_piece, count, arrived, waits)
        parts = [sums[0]]
        open_sums = None
        if c == len(chunk_rows) - 1:
            for apart in range(1, subs):
                parts.append(swapped(sums[apart], "subtree", apart))
        else:
            held = dict(enumerate(sums))
            open_sums = (held, *send(held, 1))
        pieces.append(parts)
    out = pl.pallas_call(
        functools.partial(finish_kernel, chunk_rows, [len(parts) for parts in pieces]),
        out_shape=jax.ShapeDtypeStruct((1, ANC_DEV, per_piece, block, block), jnp.float32),
        in_specs=[vmem_spec()] * sum(len(parts) for parts in pieces),
        out_specs=vmem_spec(),
        compiler_params=params,
    )(*[part for parts in pieces for part in parts])
    return out.reshape(1, ANC_DEV, per_piece * block, block)


def per_device_halving(panels, pattern, child_map, ancestor_map):
    row_total = panels.shape[2]
    pivot_width = panels.shape[3]
    block_count = child_map.shape[2]
    block_rows = row_total // block_count
    blocks = panels[0, 0].reshape(block_count, block_rows, pivot_width)
    one_hot = child_map[0, 0][:, None] == jnp.arange(block_count, dtype=jnp.int32)[None, :]
    reordered = jnp.einsum(
        "im,ipk->mpk", one_hot.astype(jnp.bfloat16), blocks, preferred_element_type=jnp.float32
    ).astype(jnp.bfloat16)
    flat_rows = reordered.reshape(row_total, pivot_width)
    hot_float = one_hot.astype(jnp.float32)
    moved_pattern = jnp.dot(
        jnp.dot(hot_float.T, pattern[0, 0].astype(jnp.float32), precision=lax.Precision.HIGHEST),
        hot_float,
        precision=lax.Precision.HIGHEST,
    )
    update = lax.dot_general(
        flat_rows, flat_rows, (((1,), (1,)), ((), ())), preferred_element_type=jnp.float32
    )
    update = (
        update.reshape(block_count, block_rows, block_count, block_rows)
        * moved_pattern[:, None, :, None]
    ).reshape(row_total, row_total)
    sub_count = lax.axis_size("subtree")
    depth = sub_count.bit_length() - 1
    my_index = lax.axis_index("subtree")
    holding = update
    for depth_step in range(depth):
        bit_number = depth - 1 - depth_step
        half_rows = holding.shape[0] // 2
        low_half = holding[:half_rows]
        high_half = holding[half_rows:]
        high_side = my_index >> bit_number & 1 == 1
        kept_half = jnp.where(high_side, high_half, low_half)
        sent_half = jnp.where(high_side, low_half, high_half)
        holding = kept_half + swapped(sent_half, "subtree", 1 << bit_number)
    piece_rows = holding.shape[0]
    column_blocks = holding.reshape(piece_rows, block_count, block_rows).transpose(1, 0, 2)
    slot_values = ancestor_map[0, 0]
    tree_count = lax.axis_size("forest")
    every_slot = lax.all_gather(slot_values, "forest", axis=0, tiled=True)
    owner_of = slot_values // ANC_DEV
    owner_hot = (owner_of[:, None] == jnp.arange(tree_count, dtype=jnp.int32)[None, :]).astype(
        jnp.float32
    )
    outgoing = jnp.einsum("co,cpq->opq", owner_hot, column_blocks, precision=lax.Precision.HIGHEST)
    incoming = lax.all_to_all(outgoing, "forest", split_axis=0, concat_axis=0, tiled=True)
    forest_index = lax.axis_index("forest")
    every_slot = every_slot.reshape(tree_count, block_count)
    mine_mask = every_slot // ANC_DEV == forest_index
    local_slot = every_slot % ANC_DEV
    source_hot = jnp.sum(
        jnp.where(
            mine_mask[:, :, None],
            (local_slot[:, :, None] == jnp.arange(ANC_DEV, dtype=jnp.int32)[None, None, :]).astype(
                jnp.float32
            ),
            0.0,
        ),
        axis=1,
    )
    summed = jnp.einsum("sk,spq->kpq", source_hot, incoming, precision=lax.Precision.HIGHEST)
    return summed[None]


def solution(mesh):
    in_specs = (
        P("subtree", "forest", None, None),
        P("subtree", "forest", None, None),
        P("subtree", "forest", None),
        P("subtree", "forest", None),
    )
    out_specs = P("subtree", "forest", None, None)

    def per_device(panels, pattern, child_map, ancestor_map):
        nb = child_map.shape[2]
        subs, trees = mesh.shape["subtree"], mesh.shape["forest"]
        if nb == trees and nb % subs == 0 and subs < META and trees % 2 == 0:
            return per_device_blocks(panels, pattern, child_map, ancestor_map)
        return per_device_halving(panels, pattern, child_map, ancestor_map)

    return jax.shard_map(
        per_device, mesh=mesh, in_specs=in_specs, out_specs=out_specs, check_vma=False
    )
```

```python
import functools

import jax
import jax.numpy as jnp
from jax import lax
from jax.experimental import pallas as pl
from jax.experimental.pallas import tpu as pltpu
from jax.sharding import PartitionSpec as P

ANC_DEV = 3
META = 8
CUT = 8
CHUNK_PARTS = (4, 4, 4, 4)
DEPS = ((1,), (1,), (2,))
ZDEP = 2
DIRECT = 1
GATHER_COST = 128 * 1024 * 1024
VMEM_LIMIT = 44 * 1024 * 1024


def swapped(shard, axis, apart):
    return lax.ppermute(shard, axis, [(i, i ^ apart) for i in range(lax.axis_size(axis))])


def smem_spec():
    return pl.BlockSpec(memory_space=pltpu.SMEM)


def vmem_spec():
    return pl.BlockSpec(memory_space=pltpu.VMEM)


def place_of(position, per_piece, my_sub):
    return ((position // per_piece) ^ my_sub) * per_piece + position % per_piece


def multiply_kernel(nb, per_piece, spans, child_any, pattern_any, map_any, panel_any, *refs):
    out_refs = refs[: len(spans)]
    plan_ref, panel_ref, child_ref, pattern_ref, map_ref, sems = refs[len(spans) :]
    block = panel_any.shape[0] // nb
    small = [
        pltpu.make_async_copy(child_any, child_ref, sems.at[nb]),
        pltpu.make_async_copy(pattern_any, pattern_ref, sems.at[nb + 1]),
        pltpu.make_async_copy(map_any, map_ref, sems.at[nb + 2]),
    ]
    for copy in small:
        copy.start()
    large = []
    for i in range(nb):
        rows = pl.ds(i * block, block)
        large.append(pltpu.make_async_copy(panel_any.at[rows, :], panel_ref.at[rows, :], sems.at[i]))
        large[-1].start()
    for copy in small:
        copy.wait()
    my_sub = lax.axis_index("subtree")
    columns = [child_ref[0, 0, i] for i in range(nb)]
    places = [place_of(column, per_piece, my_sub) for column in columns]
    empty = jnp.int32(nb)
    for i in range(nb):
        empty = jnp.where((pattern_ref[0, 0, i, i] == 0) & (places[i] < empty), places[i], empty)
    kept = []
    for i in range(nb):
        kept.append(jnp.where(places[i] == empty, nb - 1, places[i] - (places[i] > empty).astype(jnp.int32)))
        plan_ref[0, i] = map_ref[0, 0, i]
        plan_ref[1, i] = empty

    def put(i, j, value):
        for out_ref, (start, count) in zip(out_refs, spans):
            out_ref[columns[j], pl.ds(pl.multiple_of(kept[i] * count, CUT), count), :] = value[start : start + count]

    for copy in large:
        copy.wait()
    for first in range(nb - 2, -1, -2):
        product = lax.dot_general(
            panel_ref[pl.ds(first * block, (nb - first) * block), :],
            panel_ref[pl.ds(first * block, 2 * block), :],
            (((1,), (1,)), ((), ())),
            preferred_element_type=jnp.float32,
        )
        for i in range(first, nb):
            for j in (first, first + 1):
                scale = pattern_ref[0, 0, i, j].astype(jnp.float32)
                value = (
                    product[(i - first) * block : (i - first + 1) * block, (j - first) * block : (j - first + 1) * block]
                    * scale
                )
                put(i, j, value)
                if i > first + 1:
                    put(j, i, value.T)


def route_kernel(nb, per_piece, subs, shipments, counts, extra, plan_ref, *refs):
    slot_refs = refs[: subs - 1]
    update_refs = refs[subs - 1 : subs - 1 + len(counts)]
    out_ref, goal = refs[subs - 1 + len(counts) + extra :]
    block = out_ref.shape[2]
    my_tree = lax.axis_index("forest")
    half = out_ref.shape[0] // 2
    empty = plan_ref[1, 0]
    tails = []
    at = 0
    for shipment in shipments:
        tails.append(at + shipment_rows(shipment, counts) - META)
        at = tails[-1] + META
    for tail in tails:
        out_ref[:, pl.ds(tail, META), :] = jnp.full((out_ref.shape[0], META, block), empty.astype(jnp.float32))
    for apart in range(subs):
        for c in range(nb):
            entry = plan_ref[0, c] if apart == 0 else slot_refs[apart - 1][0, 0, c]
            owner = lax.div(entry, ANC_DEV)
            to = owner ^ my_tree
            to = (to & 1) * half + (to >> 1)
            goal[apart, c] = to
            slot = (entry - owner * ANC_DEV).astype(jnp.float32)
            for tail in tails:
                out_ref[to, pl.ds(tail + 1 + apart, 1), :] = jnp.full((1, block), slot, jnp.float32)
    at = 0
    for kept, chunks in shipments:
        for k in kept:
            place = k + (empty <= k).astype(jnp.int32)
            apart = place // per_piece
            for chunk in chunks:
                for c in range(nb):
                    out_ref[goal[apart, c], pl.ds(at, counts[chunk]), :] = update_refs[chunk][
                        c, pl.ds(k * counts[chunk], counts[chunk]), :
                    ]
                at += counts[chunk]
        at += META


def shipment_rows(shipment, counts):
    kept, chunks = shipment
    return len(kept) * sum(counts[chunk] for chunk in chunks) + META


def places_in(kept, nb, per_piece):
    found = {}
    for place in range(nb):
        if place in kept or place - 1 in kept:
            found.setdefault(place // per_piece, []).append(place)
    return found


def gather_kernel(nb, per_piece, kept, count, extra, *refs):
    found = places_in(kept, nb, per_piece)
    in_refs, out_refs = refs[: len(refs) - len(found) - extra], refs[-len(found) :]
    tail = len(kept) * count
    block = in_refs[0].shape[-1]
    sources = []
    for ref in in_refs:
        for index in range(ref.shape[0]):
            sources.append(ref.at[index])
    for out_ref, (apart, places) in zip(out_refs, found.items()):
        for part, place in enumerate(places):
            sums = [jnp.zeros((count, block), jnp.float32) for _ in range(ANC_DEV)]
            for source in sources:
                empty = source[pl.ds(tail, 1), :]
                slot = source[pl.ds(tail + 1 + apart, 1), :]
                value = jnp.zeros((count, block), jnp.float32)
                if place in kept:
                    value = jnp.where(empty > place, source[pl.ds(kept.index(place) * count, count), :], value)
                if place - 1 in kept:
                    value = jnp.where(empty < place, source[pl.ds(kept.index(place - 1) * count, count), :], value)
                for index in range(ANC_DEV):
                    sums[index] += jnp.where(slot == index, value, 0.0)
            for index in range(ANC_DEV):
                out_ref[index, part] = sums[index]


def pick_kernel(first, in_ref, *refs):
    refs[-1][...] = in_ref[first:]


def pick(params, blocks, first, earlier):
    return pl.pallas_call(
        functools.partial(pick_kernel, first),
        out_shape=jax.ShapeDtypeStruct((blocks.shape[0] - first, *blocks.shape[1:]), blocks.dtype),
        in_specs=[vmem_spec()] + [pl.BlockSpec(memory_space=pl.ANY)] * len(earlier),
        out_specs=vmem_spec(),
        compiler_params=params,
    )(blocks, *earlier)


def pack_kernel(chip, same_ref, crossed_ref, *refs):
    refs[-1][0] = same_ref[chip]
    refs[-1][1] = crossed_ref[chip]


def pack(params, chip, same, crossed, *earlier):
    return pl.pallas_call(
        functools.partial(pack_kernel, chip),
        out_shape=jax.ShapeDtypeStruct((2, *same.shape[1:]), jnp.float32),
        in_specs=[vmem_spec()] * 2 + [pl.BlockSpec(memory_space=pl.ANY)] * len(earlier),
        out_specs=vmem_spec(),
        compiler_params=params,
    )(same, crossed, *earlier)


def gather(params, nb, per_piece, kept, arrived, earlier):
    block = arrived[0].shape[-1]
    count = (arrived[0].shape[1] - META) // len(kept)
    found = places_in(kept, nb, per_piece)
    return pl.pallas_call(
        functools.partial(gather_kernel, nb, per_piece, kept, count, len(earlier)),
        out_shape=[jax.ShapeDtypeStruct((ANC_DEV, len(places), count, block), jnp.float32) for places in found.values()],
        in_specs=[vmem_spec()] * len(arrived) + [pl.BlockSpec(memory_space=pl.ANY)] * len(earlier),
        out_specs=[vmem_spec()] * len(found),
        compiler_params=params,
        cost_estimate=pl.CostEstimate(flops=0, bytes_accessed=GATHER_COST, transcendentals=0),
    )(*arrived, *earlier)


def add_kernel(places, *refs):
    came_ref, out_refs = refs[len(places)], refs[-len(places) :]
    for held_ref, place, out_ref in zip(refs, places, out_refs):
        out_ref[...] = held_ref[...] + came_ref[place]


def send(held, apart):
    going = [index for index in held if index & apart]
    return going, swapped(jnp.stack([held[index] for index in going]), "subtree", apart)


def settle(params, held, parts, apart, going, came, earlier):
    parts.append(came[going.index(apart)])
    for index in going:
        del held[index]
    kept = [index ^ apart for index in going if index != apart]
    if kept:
        sums = pl.pallas_call(
            functools.partial(add_kernel, [going.index(index ^ apart) for index in kept]),
            out_shape=[jax.ShapeDtypeStruct(came.shape[1:], came.dtype)] * len(kept),
            in_specs=[vmem_spec()] * (len(kept) + 1) + [pl.BlockSpec(memory_space=pl.ANY)] * len(earlier),
            out_specs=[vmem_spec()] * len(kept),
            compiler_params=params,
        )(*[held[index] for index in kept], came, *earlier)
        held.update(zip(kept, sums))


def finish_kernel(chunk_rows, shares, near_ref, *refs):
    out_ref = refs[-1]
    start = at = 0
    for count, share in zip(chunk_rows, shares):
        rows = pl.ds(start, count)
        for part in range(out_ref.shape[2]):
            total = refs[at + 1][:, part]
            for came in refs[at + 2 : at + share]:
                total += came[:, part]
            if part < near_ref.shape[1]:
                total += near_ref[:, part, rows]
            if part > 0:
                total += refs[at][:, part - 1]
            out_ref[0, :, part, rows, :] = total
        start += count
        at += share


def per_device_blocks(panels, pattern, child_map, ancestor_map):
    row_total, pivot_width = panels.shape[2:]
    nb = child_map.shape[2]
    block = row_total // nb
    subs = lax.axis_size("subtree")
    trees = lax.axis_size("forest")
    per_piece = nb // subs
    units = block // CUT
    chunk_rows = []
    for index, share in enumerate(CHUNK_PARTS):
        chunk_rows.append(units * share // sum(CHUNK_PARTS) * CUT)
    chunk_rows[-1] += block - sum(chunk_rows)
    chips = trees // 2
    params = pltpu.CompilerParams(vmem_limit_bytes=VMEM_LIMIT)

    panel = panels.reshape(row_total, pivot_width)
    spans = []
    for count in chunk_rows:
        spans.append((sum(chunk_rows[: len(spans)]), count))
    slots = [swapped(ancestor_map, "subtree", apart) for apart in range(1, subs)]
    updates = pl.pallas_call(
        functools.partial(multiply_kernel, nb, per_piece, spans),
        out_shape=[jax.ShapeDtypeStruct((nb, nb * count, block), jnp.float32) for count in chunk_rows]
        + [jax.ShapeDtypeStruct((2, nb), jnp.int32)],
        in_specs=[pl.BlockSpec(memory_space=pltpu.HBM)] * 4,
        out_specs=[vmem_spec()] * len(spans) + [smem_spec()],
        scratch_shapes=[
            pltpu.VMEM((row_total, pivot_width), jnp.bfloat16),
            pltpu.SMEM(child_map.shape, jnp.int32),
            pltpu.SMEM(pattern.shape, jnp.int32),
            pltpu.SMEM(ancestor_map.shape, jnp.int32),
            pltpu.SemaphoreType.DMA((nb + 3,)),
        ],
        compiler_params=params,
        cost_estimate=pl.CostEstimate(
            flops=2 * nb * block * row_total * pivot_width,
            bytes_accessed=2 * row_total * pivot_width,
            transcendentals=0,
        ),
    )(*[pltpu.with_memory_space_constraint(array, pltpu.HBM) for array in (child_map, pattern, ancestor_map, panel)])
    plan = updates[-1]
    far = list(range(1, nb - 1))
    shipments = [(far, [chunk]) for chunk in range(len(chunk_rows))]
    shipments.append(([0], list(range(len(chunk_rows)))))
    laid = []
    earlier = []
    for group in (shipments[:1], shipments[1:]):
        used = chunk_rows[:1] if not laid else chunk_rows
        rows = [shipment_rows(shipment, chunk_rows) for shipment in group]
        blocks = pl.pallas_call(
            functools.partial(route_kernel, nb, per_piece, subs, group, used, len(earlier)),
            out_shape=jax.ShapeDtypeStruct((trees, sum(rows), block), jnp.float32),
            in_specs=[smem_spec()] * subs
            + [vmem_spec()] * len(used)
            + [pl.BlockSpec(memory_space=pl.ANY)] * len(earlier),
            out_specs=vmem_spec(),
            scratch_shapes=[pltpu.SMEM((subs, nb), jnp.int32)],
            compiler_params=params,
        )(plan, *slots, *updates[: len(used)], *earlier)
        other = blocks[chips:] if not laid else pick(params, blocks, chips, going_out)
        same, crossed = blocks[:chips], swapped(other, "forest", 1)
        at = 0
        for count in rows:
            laid.append((same[:, at : at + count], crossed[:, at : at + count]))
            at += count
        if not earlier:
            going_out = [pack(params, chip, *laid[0]) for chip in range(1, chips)]
            earlier = [blocks]

    pieces = []
    open_sums = None
    for c, (kept, _) in enumerate(shipments):
        arrived = [laid[c][0][:1], laid[c][1][:1]]
        for chip in range(1, chips):
            arrived.append(swapped(going_out[chip - 1], "forest", 2 * chip))
        last = c == len(shipments) - 1
        queued = []
        waits = []
        for chip in range(1, chips):
            if open_sums is not None and chip == chips - 1:
                held, apart = open_sums[0], 1
                settle(params, held, pieces[-1], apart, *open_sums[1:], waits)
                waits = waits + list(held.values())[1:]
                while 2 * apart < subs:
                    apart *= 2
                    settle(params, held, pieces[-1], apart, *send(held, apart), [])
            if not last:
                earlier = [arrived[index + 1] for index in DEPS[chip - 1]]
                if chip == 2 and c > 1 and ZDEP:
                    earlier.append(pieces[c - 2][-1])
                if chip == chips - 1:
                    earlier += waits[chip - 1 :]
                queued.append(pack(params, chip, *laid[c + 1], *earlier))
                waits = waits[: chip - 1] + queued[-1:] + waits[chip - 1 :]
        going_out = queued
        sums = gather(params, nb, per_piece, kept, arrived, waits)
        if last:
            near = sums[0]
            break
        parts = [sums[0]]
        open_sums = None
        if c == len(chunk_rows) - 1 and DIRECT:
            for apart in range(1, subs):
                parts.append(swapped(sums[apart], "subtree", apart))
        else:
            held = dict(enumerate(sums))
            open_sums = (held, *send(held, 1))
        pieces.append(parts)
    out = pl.pallas_call(
        functools.partial(finish_kernel, chunk_rows, [len(parts) for parts in pieces]),
        out_shape=jax.ShapeDtypeStruct((1, ANC_DEV, per_piece, block, block), jnp.float32),
        in_specs=[vmem_spec()] * (1 + sum(len(parts) for parts in pieces)),
        out_specs=vmem_spec(),
        compiler_params=params,
    )(near, *[part for parts in pieces for part in parts])
    return out.reshape(1, ANC_DEV, per_piece * block, block)


def per_device_halving(panels, pattern, child_map, ancestor_map):
    row_total = panels.shape[2]
    pivot_width = panels.shape[3]
    block_count = child_map.shape[2]
    block_rows = row_total // block_count
    blocks = panels[0, 0].reshape(block_count, block_rows, pivot_width)
    one_hot = child_map[0, 0][:, None] == jnp.arange(block_count, dtype=jnp.int32)[None, :]
    reordered = jnp.einsum(
        "im,ipk->mpk", one_hot.astype(jnp.bfloat16), blocks, preferred_element_type=jnp.float32
    ).astype(jnp.bfloat16)
    flat_rows = reordered.reshape(row_total, pivot_width)
    hot_float = one_hot.astype(jnp.float32)
    moved_pattern = jnp.dot(
        jnp.dot(hot_float.T, pattern[0, 0].astype(jnp.float32), precision=lax.Precision.HIGHEST),
        hot_float,
        precision=lax.Precision.HIGHEST,
    )
    update = lax.dot_general(
        flat_rows, flat_rows, (((1,), (1,)), ((), ())), preferred_element_type=jnp.float32
    )
    update = (
        update.reshape(block_count, block_rows, block_count, block_rows)
        * moved_pattern[:, None, :, None]
    ).reshape(row_total, row_total)
    sub_count = lax.axis_size("subtree")
    depth = sub_count.bit_length() - 1
    my_index = lax.axis_index("subtree")
    holding = update
    for depth_step in range(depth):
        bit_number = depth - 1 - depth_step
        half_rows = holding.shape[0] // 2
        low_half = holding[:half_rows]
        high_half = holding[half_rows:]
        high_side = my_index >> bit_number & 1 == 1
        kept_half = jnp.where(high_side, high_half, low_half)
        sent_half = jnp.where(high_side, low_half, high_half)
        holding = kept_half + swapped(sent_half, "subtree", 1 << bit_number)
    piece_rows = holding.shape[0]
    column_blocks = holding.reshape(piece_rows, block_count, block_rows).transpose(1, 0, 2)
    slot_values = ancestor_map[0, 0]
    tree_count = lax.axis_size("forest")
    every_slot = lax.all_gather(slot_values, "forest", axis=0, tiled=True)
    owner_of = slot_values // ANC_DEV
    owner_hot = (owner_of[:, None] == jnp.arange(tree_count, dtype=jnp.int32)[None, :]).astype(
        jnp.float32
    )
    outgoing = jnp.einsum("co,cpq->opq", owner_hot, column_blocks, precision=lax.Precision.HIGHEST)
    incoming = lax.all_to_all(outgoing, "forest", split_axis=0, concat_axis=0, tiled=True)
    forest_index = lax.axis_index("forest")
    every_slot = every_slot.reshape(tree_count, block_count)
    mine_mask = every_slot // ANC_DEV == forest_index
    local_slot = every_slot % ANC_DEV
    source_hot = jnp.sum(
        jnp.where(
            mine_mask[:, :, None],
            (local_slot[:, :, None] == jnp.arange(ANC_DEV, dtype=jnp.int32)[None, None, :]).astype(
                jnp.float32
            ),
            0.0,
        ),
        axis=1,
    )
    summed = jnp.einsum("sk,spq->kpq", source_hot, incoming, precision=lax.Precision.HIGHEST)
    return summed[None]


def solution(mesh):
    in_specs = (
        P("subtree", "forest", None, None),
        P("subtree", "forest", None, None),
        P("subtree", "forest", None),
        P("subtree", "forest", None),
    )
    out_specs = P("subtree", "forest", None, None)

    def per_device(panels, pattern, child_map, ancestor_map):
        nb = child_map.shape[2]
        subs, trees = mesh.shape["subtree"], mesh.shape["forest"]
        if nb == trees and nb % (2 * subs) == 0 and subs < META:
            return per_device_blocks(panels, pattern, child_map, ancestor_map)
        return per_device_halving(panels, pattern, child_map, ancestor_map)

    return jax.shard_map(
        per_device, mesh=mesh, in_specs=in_specs, out_specs=out_specs, check_vma=False
    )
```

```python
import functools

import jax
import jax.numpy as jnp
from jax import lax
from jax.experimental import pallas as pl
from jax.experimental.pallas import tpu as pltpu
from jax.sharding import PartitionSpec as P

ANC_DEV = 3
META = 8
CUT = 8
CHUNK_PARTS = (3, 4, 4, 5)
DEPS = ((1,), (1,), (2,))
ZDEP = 2
DIRECT = 1
GATHER_COST = 128 * 1024 * 1024
VMEM_LIMIT = 44 * 1024 * 1024


def swapped(shard, axis, apart):
    return lax.ppermute(shard, axis, [(i, i ^ apart) for i in range(lax.axis_size(axis))])


def smem_spec():
    return pl.BlockSpec(memory_space=pltpu.SMEM)


def vmem_spec():
    return pl.BlockSpec(memory_space=pltpu.VMEM)


def place_of(position, per_piece, my_sub):
    return ((position // per_piece) ^ my_sub) * per_piece + position % per_piece


def multiply_kernel(nb, per_piece, spans, child_any, pattern_any, map_any, panel_any, *refs):
    out_refs = refs[: len(spans)]
    plan_ref, panel_ref, child_ref, pattern_ref, map_ref, sems = refs[len(spans) :]
    block = panel_any.shape[0] // nb
    small = [
        pltpu.make_async_copy(child_any, child_ref, sems.at[nb]),
        pltpu.make_async_copy(pattern_any, pattern_ref, sems.at[nb + 1]),
        pltpu.make_async_copy(map_any, map_ref, sems.at[nb + 2]),
    ]
    for copy in small:
        copy.start()
    large = []
    for i in range(nb):
        rows = pl.ds(i * block, block)
        large.append(pltpu.make_async_copy(panel_any.at[rows, :], panel_ref.at[rows, :], sems.at[i]))
        large[-1].start()
    for copy in small:
        copy.wait()
    my_sub = lax.axis_index("subtree")
    columns = [child_ref[0, 0, i] for i in range(nb)]
    places = [place_of(column, per_piece, my_sub) for column in columns]
    empty = jnp.int32(nb)
    for i in range(nb):
        empty = jnp.where((pattern_ref[0, 0, i, i] == 0) & (places[i] < empty), places[i], empty)
    kept = []
    for i in range(nb):
        kept.append(jnp.where(places[i] == empty, nb - 1, places[i] - (places[i] > empty).astype(jnp.int32)))
        plan_ref[0, i] = map_ref[0, 0, i]
        plan_ref[1, i] = empty

    def put(i, j, value):
        for out_ref, (start, count) in zip(out_refs, spans):
            out_ref[columns[j], pl.ds(pl.multiple_of(kept[i] * count, CUT), count), :] = value[start : start + count]

    for copy in large:
        copy.wait()
    for first in range(nb - 2, -1, -2):
        product = lax.dot_general(
            panel_ref[pl.ds(first * block, (nb - first) * block), :],
            panel_ref[pl.ds(first * block, 2 * block), :],
            (((1,), (1,)), ((), ())),
            preferred_element_type=jnp.float32,
        )
        for i in range(first, nb):
            for j in (first, first + 1):
                scale = pattern_ref[0, 0, i, j].astype(jnp.float32)
                value = (
                    product[(i - first) * block : (i - first + 1) * block, (j - first) * block : (j - first + 1) * block]
                    * scale
                )
                put(i, j, value)
                if i > first + 1:
                    put(j, i, value.T)


def route_kernel(nb, per_piece, subs, shipments, counts, extra, plan_ref, *refs):
    slot_refs = refs[: subs - 1]
    update_refs = refs[subs - 1 : subs - 1 + len(counts)]
    out_ref, goal = refs[subs - 1 + len(counts) + extra :]
    block = out_ref.shape[2]
    my_tree = lax.axis_index("forest")
    half = out_ref.shape[0] // 2
    empty = plan_ref[1, 0]
    tails = []
    at = 0
    for shipment in shipments:
        tails.append(at + shipment_rows(shipment, counts) - META)
        at = tails[-1] + META
    for tail in tails:
        out_ref[:, pl.ds(tail, META), :] = jnp.full((out_ref.shape[0], META, block), empty.astype(jnp.float32))
    for apart in range(subs):
        for c in range(nb):
            entry = plan_ref[0, c] if apart == 0 else slot_refs[apart - 1][0, 0, c]
            owner = lax.div(entry, ANC_DEV)
            to = owner ^ my_tree
            to = (to & 1) * half + (to >> 1)
            goal[apart, c] = to
            slot = (entry - owner * ANC_DEV).astype(jnp.float32)
            for tail in tails:
                out_ref[to, pl.ds(tail + 1 + apart, 1), :] = jnp.full((1, block), slot, jnp.float32)
    at = 0
    for kept, chunks in shipments:
        for k in kept:
            place = k + (empty <= k).astype(jnp.int32)
            apart = place // per_piece
            for chunk in chunks:
                for c in range(nb):
                    out_ref[goal[apart, c], pl.ds(at, counts[chunk]), :] = update_refs[chunk][
                        c, pl.ds(k * counts[chunk], counts[chunk]), :
                    ]
                at += counts[chunk]
        at += META


def shipment_rows(shipment, counts):
    kept, chunks = shipment
    return len(kept) * sum(counts[chunk] for chunk in chunks) + META


def places_in(kept, nb, per_piece):
    found = {}
    for place in range(nb):
        if place in kept or place - 1 in kept:
            found.setdefault(place // per_piece, []).append(place)
    return found


def gather_kernel(nb, per_piece, kept, count, extra, *refs):
    found = places_in(kept, nb, per_piece)
    in_refs, out_refs = refs[: len(refs) - len(found) - extra], refs[-len(found) :]
    tail = len(kept) * count
    block = in_refs[0].shape[-1]
    sources = []
    for ref in in_refs:
        for index in range(ref.shape[0]):
            sources.append(ref.at[index])
    for out_ref, (apart, places) in zip(out_refs, found.items()):
        for part, place in enumerate(places):
            sums = [jnp.zeros((count, block), jnp.float32) for _ in range(ANC_DEV)]
            for source in sources:
                empty = source[pl.ds(tail, 1), :]
                slot = source[pl.ds(tail + 1 + apart, 1), :]
                value = jnp.zeros((count, block), jnp.float32)
                if place in kept:
                    value = jnp.where(empty > place, source[pl.ds(kept.index(place) * count, count), :], value)
                if place - 1 in kept:
                    value = jnp.where(empty < place, source[pl.ds(kept.index(place - 1) * count, count), :], value)
                for index in range(ANC_DEV):
                    sums[index] += jnp.where(slot == index, value, 0.0)
            for index in range(ANC_DEV):
                out_ref[index, part] = sums[index]


def pick_kernel(first, in_ref, *refs):
    refs[-1][...] = in_ref[first:]


def pick(params, blocks, first, earlier):
    return pl.pallas_call(
        functools.partial(pick_kernel, first),
        out_shape=jax.ShapeDtypeStruct((blocks.shape[0] - first, *blocks.shape[1:]), blocks.dtype),
        in_specs=[vmem_spec()] + [pl.BlockSpec(memory_space=pl.ANY)] * len(earlier),
        out_specs=vmem_spec(),
        compiler_params=params,
    )(blocks, *earlier)


def pack_kernel(chip, same_ref, crossed_ref, *refs):
    refs[-1][0] = same_ref[chip]
    refs[-1][1] = crossed_ref[chip]


def pack(params, chip, same, crossed, *earlier):
    return pl.pallas_call(
        functools.partial(pack_kernel, chip),
        out_shape=jax.ShapeDtypeStruct((2, *same.shape[1:]), jnp.float32),
        in_specs=[vmem_spec()] * 2 + [pl.BlockSpec(memory_space=pl.ANY)] * len(earlier),
        out_specs=vmem_spec(),
        compiler_params=params,
    )(same, crossed, *earlier)


def gather(params, nb, per_piece, kept, arrived, earlier):
    block = arrived[0].shape[-1]
    count = (arrived[0].shape[1] - META) // len(kept)
    found = places_in(kept, nb, per_piece)
    return pl.pallas_call(
        functools.partial(gather_kernel, nb, per_piece, kept, count, len(earlier)),
        out_shape=[jax.ShapeDtypeStruct((ANC_DEV, len(places), count, block), jnp.float32) for places in found.values()],
        in_specs=[vmem_spec()] * len(arrived) + [pl.BlockSpec(memory_space=pl.ANY)] * len(earlier),
        out_specs=[vmem_spec()] * len(found),
        compiler_params=params,
        cost_estimate=pl.CostEstimate(flops=0, bytes_accessed=GATHER_COST, transcendentals=0),
    )(*arrived, *earlier)


def add_kernel(places, *refs):
    came_ref, out_refs = refs[len(places)], refs[-len(places) :]
    for held_ref, place, out_ref in zip(refs, places, out_refs):
        out_ref[...] = held_ref[...] + came_ref[place]


def send(held, apart):
    going = [index for index in held if index & apart]
    return going, swapped(jnp.stack([held[index] for index in going]), "subtree", apart)


def settle(params, held, parts, apart, going, came, earlier):
    parts.append(came[going.index(apart)])
    for index in going:
        del held[index]
    kept = [index ^ apart for index in going if index != apart]
    if kept:
        sums = pl.pallas_call(
            functools.partial(add_kernel, [going.index(index ^ apart) for index in kept]),
            out_shape=[jax.ShapeDtypeStruct(came.shape[1:], came.dtype)] * len(kept),
            in_specs=[vmem_spec()] * (len(kept) + 1) + [pl.BlockSpec(memory_space=pl.ANY)] * len(earlier),
            out_specs=[vmem_spec()] * len(kept),
            compiler_params=params,
        )(*[held[index] for index in kept], came, *earlier)
        held.update(zip(kept, sums))


def finish_kernel(chunk_rows, shares, near_ref, *refs):
    out_ref = refs[-1]
    start = at = 0
    for count, share in zip(chunk_rows, shares):
        rows = pl.ds(start, count)
        for part in range(out_ref.shape[2]):
            total = refs[at + 1][:, part]
            for came in refs[at + 2 : at + share]:
                total += came[:, part]
            if part < near_ref.shape[1]:
                total += near_ref[:, part, rows]
            if part > 0:
                total += refs[at][:, part - 1]
            out_ref[0, :, part, rows, :] = total
        start += count
        at += share


def per_device_blocks(panels, pattern, child_map, ancestor_map):
    row_total, pivot_width = panels.shape[2:]
    nb = child_map.shape[2]
    block = row_total // nb
    subs = lax.axis_size("subtree")
    trees = lax.axis_size("forest")
    per_piece = nb // subs
    units = block // CUT
    chunk_rows = []
    for index, share in enumerate(CHUNK_PARTS):
        chunk_rows.append(units * share // sum(CHUNK_PARTS) * CUT)
    chunk_rows[-1] += block - sum(chunk_rows)
    chips = trees // 2
    params = pltpu.CompilerParams(vmem_limit_bytes=VMEM_LIMIT)

    panel = panels.reshape(row_total, pivot_width)
    spans = []
    for count in chunk_rows:
        spans.append((sum(chunk_rows[: len(spans)]), count))
    slots = [swapped(ancestor_map, "subtree", apart) for apart in range(1, subs)]
    updates = pl.pallas_call(
        functools.partial(multiply_kernel, nb, per_piece, spans),
        out_shape=[jax.ShapeDtypeStruct((nb, nb * count, block), jnp.float32) for count in chunk_rows]
        + [jax.ShapeDtypeStruct((2, nb), jnp.int32)],
        in_specs=[pl.BlockSpec(memory_space=pltpu.HBM)] * 4,
        out_specs=[vmem_spec()] * len(spans) + [smem_spec()],
        scratch_shapes=[
            pltpu.VMEM((row_total, pivot_width), jnp.bfloat16),
            pltpu.SMEM(child_map.shape, jnp.int32),
            pltpu.SMEM(pattern.shape, jnp.int32),
            pltpu.SMEM(ancestor_map.shape, jnp.int32),
            pltpu.SemaphoreType.DMA((nb + 3,)),
        ],
        compiler_params=params,
        cost_estimate=pl.CostEstimate(
            flops=2 * nb * block * row_total * pivot_width,
            bytes_accessed=2 * row_total * pivot_width,
            transcendentals=0,
        ),
    )(*[pltpu.with_memory_space_constraint(array, pltpu.HBM) for array in (child_map, pattern, ancestor_map, panel)])
    plan = updates[-1]
    far = list(range(1, nb - 1))
    shipments = [(far, [chunk]) for chunk in range(len(chunk_rows))]
    shipments.append(([0], list(range(len(chunk_rows)))))
    laid = []
    earlier = []
    for group in (shipments[:1], shipments[1:]):
        used = chunk_rows[:1] if not laid else chunk_rows
        rows = [shipment_rows(shipment, chunk_rows) for shipment in group]
        blocks = pl.pallas_call(
            functools.partial(route_kernel, nb, per_piece, subs, group, used, len(earlier)),
            out_shape=jax.ShapeDtypeStruct((trees, sum(rows), block), jnp.float32),
            in_specs=[smem_spec()] * subs
            + [vmem_spec()] * len(used)
            + [pl.BlockSpec(memory_space=pl.ANY)] * len(earlier),
            out_specs=vmem_spec(),
            scratch_shapes=[pltpu.SMEM((subs, nb), jnp.int32)],
            compiler_params=params,
        )(plan, *slots, *updates[: len(used)], *earlier)
        other = blocks[chips:] if not laid else pick(params, blocks, chips, going_out)
        same, crossed = blocks[:chips], swapped(other, "forest", 1)
        at = 0
        for count in rows:
            laid.append((same[:, at : at + count], crossed[:, at : at + count]))
            at += count
        if not earlier:
            going_out = [pack(params, chip, *laid[0]) for chip in range(1, chips)]
            earlier = [blocks]

    pieces = []
    open_sums = None
    for c, (kept, _) in enumerate(shipments):
        arrived = [laid[c][0][:1], laid[c][1][:1]]
        for chip in range(1, chips):
            arrived.append(swapped(going_out[chip - 1], "forest", 2 * chip))
        last = c == len(shipments) - 1
        queued = []
        waits = []
        for chip in range(1, chips):
            if open_sums is not None and chip == chips - 1:
                held, apart = open_sums[0], 1
                settle(params, held, pieces[-1], apart, *open_sums[1:], waits)
                waits = waits + list(held.values())[1:]
                while 2 * apart < subs:
                    apart *= 2
                    settle(params, held, pieces[-1], apart, *send(held, apart), [])
            if not last:
                earlier = [arrived[index + 1] for index in DEPS[chip - 1]]
                if chip == 2 and c > 1 and ZDEP:
                    earlier.append(pieces[c - 2][-1])
                if chip == chips - 1:
                    earlier += waits[chip - 1 :]
                queued.append(pack(params, chip, *laid[c + 1], *earlier))
                waits = waits[: chip - 1] + queued[-1:] + waits[chip - 1 :]
        going_out = queued
        sums = gather(params, nb, per_piece, kept, arrived, waits)
        if last:
            near = sums[0]
            break
        parts = [sums[0]]
        open_sums = None
        if c == len(chunk_rows) - 1 and DIRECT:
            for apart in range(1, subs):
                parts.append(swapped(sums[apart], "subtree", apart))
        else:
            held = dict(enumerate(sums))
            open_sums = (held, *send(held, 1))
        pieces.append(parts)
    out = pl.pallas_call(
        functools.partial(finish_kernel, chunk_rows, [len(parts) for parts in pieces]),
        out_shape=jax.ShapeDtypeStruct((1, ANC_DEV, per_piece, block, block), jnp.float32),
        in_specs=[vmem_spec()] * (1 + sum(len(parts) for parts in pieces)),
        out_specs=vmem_spec(),
        compiler_params=params,
    )(near, *[part for parts in pieces for part in parts])
    return out.reshape(1, ANC_DEV, per_piece * block, block)


def per_device_halving(panels, pattern, child_map, ancestor_map):
    row_total = panels.shape[2]
    pivot_width = panels.shape[3]
    block_count = child_map.shape[2]
    block_rows = row_total // block_count
    blocks = panels[0, 0].reshape(block_count, block_rows, pivot_width)
    one_hot = child_map[0, 0][:, None] == jnp.arange(block_count, dtype=jnp.int32)[None, :]
    reordered = jnp.einsum(
        "im,ipk->mpk", one_hot.astype(jnp.bfloat16), blocks, preferred_element_type=jnp.float32
    ).astype(jnp.bfloat16)
    flat_rows = reordered.reshape(row_total, pivot_width)
    hot_float = one_hot.astype(jnp.float32)
    moved_pattern = jnp.dot(
        jnp.dot(hot_float.T, pattern[0, 0].astype(jnp.float32), precision=lax.Precision.HIGHEST),
        hot_float,
        precision=lax.Precision.HIGHEST,
    )
    update = lax.dot_general(
        flat_rows, flat_rows, (((1,), (1,)), ((), ())), preferred_element_type=jnp.float32
    )
    update = (
        update.reshape(block_count, block_rows, block_count, block_rows)
        * moved_pattern[:, None, :, None]
    ).reshape(row_total, row_total)
    sub_count = lax.axis_size("subtree")
    depth = sub_count.bit_length() - 1
    my_index = lax.axis_index("subtree")
    holding = update
    for depth_step in range(depth):
        bit_number = depth - 1 - depth_step
        half_rows = holding.shape[0] // 2
        low_half = holding[:half_rows]
        high_half = holding[half_rows:]
        high_side = my_index >> bit_number & 1 == 1
        kept_half = jnp.where(high_side, high_half, low_half)
        sent_half = jnp.where(high_side, low_half, high_half)
        holding = kept_half + swapped(sent_half, "subtree", 1 << bit_number)
    piece_rows = holding.shape[0]
    column_blocks = holding.reshape(piece_rows, block_count, block_rows).transpose(1, 0, 2)
    slot_values = ancestor_map[0, 0]
    tree_count = lax.axis_size("forest")
    every_slot = lax.all_gather(slot_values, "forest", axis=0, tiled=True)
    owner_of = slot_values // ANC_DEV
    owner_hot = (owner_of[:, None] == jnp.arange(tree_count, dtype=jnp.int32)[None, :]).astype(
        jnp.float32
    )
    outgoing = jnp.einsum("co,cpq->opq", owner_hot, column_blocks, precision=lax.Precision.HIGHEST)
    incoming = lax.all_to_all(outgoing, "forest", split_axis=0, concat_axis=0, tiled=True)
    forest_index = lax.axis_index("forest")
    every_slot = every_slot.reshape(tree_count, block_count)
    mine_mask = every_slot // ANC_DEV == forest_index
    local_slot = every_slot % ANC_DEV
    source_hot = jnp.sum(
        jnp.where(
            mine_mask[:, :, None],
            (local_slot[:, :, None] == jnp.arange(ANC_DEV, dtype=jnp.int32)[None, None, :]).astype(
                jnp.float32
            ),
            0.0,
        ),
        axis=1,
    )
    summed = jnp.einsum("sk,spq->kpq", source_hot, incoming, precision=lax.Precision.HIGHEST)
    return summed[None]


def solution(mesh):
    in_specs = (
        P("subtree", "forest", None, None),
        P("subtree", "forest", None, None),
        P("subtree", "forest", None),
        P("subtree", "forest", None),
    )
    out_specs = P("subtree", "forest", None, None)

    def per_device(panels, pattern, child_map, ancestor_map):
        nb = child_map.shape[2]
        subs, trees = mesh.shape["subtree"], mesh.shape["forest"]
        if nb == trees and nb % (2 * subs) == 0 and subs < META:
            return per_device_blocks(panels, pattern, child_map, ancestor_map)
        return per_device_halving(panels, pattern, child_map, ancestor_map)

    return jax.shard_map(
        per_device, mesh=mesh, in_specs=in_specs, out_specs=out_specs, check_vma=False
    )
```

```python
import functools

import jax
import jax.numpy as jnp
from jax import lax
from jax.experimental import pallas as pl
from jax.experimental.pallas import tpu as pltpu
from jax.sharding import PartitionSpec as P

ANC_DEV = 3
META = 8
CUT = 8
CHUNK_PARTS = (3, 4, 4, 5)
DEPS = ((1,), (1,), (2,))
ZDEP = 2
DIRECT = 1
GATHER_COST = 128 * 1024 * 1024
VMEM_LIMIT = 44 * 1024 * 1024


def swapped(shard, axis, apart):
    return lax.ppermute(shard, axis, [(i, i ^ apart) for i in range(lax.axis_size(axis))])


def smem_spec():
    return pl.BlockSpec(memory_space=pltpu.SMEM)


def vmem_spec():
    return pl.BlockSpec(memory_space=pltpu.VMEM)


def place_of(position, per_piece, my_sub):
    return ((position // per_piece) ^ my_sub) * per_piece + position % per_piece


def multiply_kernel(nb, per_piece, spans, child_any, pattern_any, map_any, panel_any, *refs):
    out_refs = refs[: len(spans)]
    plan_ref, panel_ref, child_ref, pattern_ref, map_ref, sems = refs[len(spans) :]
    block = panel_any.shape[0] // nb
    small = [
        pltpu.make_async_copy(child_any, child_ref, sems.at[nb]),
        pltpu.make_async_copy(pattern_any, pattern_ref, sems.at[nb + 1]),
        pltpu.make_async_copy(map_any, map_ref, sems.at[nb + 2]),
    ]
    for copy in small:
        copy.start()
    large = []
    for i in range(nb):
        rows = pl.ds(i * block, block)
        large.append(pltpu.make_async_copy(panel_any.at[rows, :], panel_ref.at[rows, :], sems.at[i]))
        large[-1].start()
    for copy in small:
        copy.wait()
    my_sub = lax.axis_index("subtree")
    columns = [child_ref[0, 0, i] for i in range(nb)]
    places = [place_of(column, per_piece, my_sub) for column in columns]
    empty = jnp.int32(nb)
    for i in range(nb):
        empty = jnp.where((pattern_ref[0, 0, i, i] == 0) & (places[i] < empty), places[i], empty)
    kept = []
    for i in range(nb):
        kept.append(jnp.where(places[i] == empty, nb - 1, places[i] - (places[i] > empty).astype(jnp.int32)))
        plan_ref[0, i] = map_ref[0, 0, i]
        plan_ref[1, i] = empty

    def put(i, j, value):
        for out_ref, (start, count) in zip(out_refs, spans):
            out_ref[columns[j], pl.ds(pl.multiple_of(kept[i] * count, CUT), count), :] = value[start : start + count]

    for copy in large:
        copy.wait()
    for first in range(nb - 2, -1, -2):
        product = lax.dot_general(
            panel_ref[pl.ds(first * block, (nb - first) * block), :],
            panel_ref[pl.ds(first * block, 2 * block), :],
            (((1,), (1,)), ((), ())),
            preferred_element_type=jnp.float32,
        )
        for i in range(first, nb):
            for j in (first, first + 1):
                scale = pattern_ref[0, 0, i, j].astype(jnp.float32)
                value = (
                    product[(i - first) * block : (i - first + 1) * block, (j - first) * block : (j - first + 1) * block]
                    * scale
                )
                put(i, j, value)
                if i > first + 1:
                    put(j, i, value.T)


def route_kernel(nb, per_piece, subs, shipments, counts, extra, plan_ref, *refs):
    slot_refs = refs[: subs - 1]
    update_refs = refs[subs - 1 : subs - 1 + len(counts)]
    out_ref, goal = refs[subs - 1 + len(counts) + extra :]
    block = out_ref.shape[2]
    my_tree = lax.axis_index("forest")
    half = out_ref.shape[0] // 2
    empty = plan_ref[1, 0]
    tails = []
    at = 0
    for shipment in shipments:
        tails.append(at + shipment_rows(shipment, counts) - META)
        at = tails[-1] + META
    for tail in tails:
        out_ref[:, pl.ds(tail, META), :] = jnp.full((out_ref.shape[0], META, block), empty.astype(jnp.float32))
    for apart in range(subs):
        for c in range(nb):
            entry = plan_ref[0, c] if apart == 0 else slot_refs[apart - 1][0, 0, c]
            owner = (entry * (65536 // ANC_DEV + 1)) >> 16
            to = owner ^ my_tree
            to = (to & 1) * half + (to >> 1)
            goal[apart, c] = to
            slot = (entry - owner * ANC_DEV).astype(jnp.float32)
            for tail in tails:
                out_ref[to, pl.ds(tail + 1 + apart, 1), :] = jnp.full((1, block), slot, jnp.float32)
    at = 0
    for kept, chunks in shipments:
        for k in kept:
            place = k + (empty <= k).astype(jnp.int32)
            apart = lax.div(place, jnp.int32(per_piece))
            for chunk in chunks:
                for c in range(nb):
                    out_ref[goal[apart, c], pl.ds(at, counts[chunk]), :] = update_refs[chunk][
                        c, pl.ds(k * counts[chunk], counts[chunk]), :
                    ]
                at += counts[chunk]
        at += META


def shipment_rows(shipment, counts):
    kept, chunks = shipment
    return len(kept) * sum(counts[chunk] for chunk in chunks) + META


def places_in(kept, nb, per_piece):
    found = {}
    for place in range(nb):
        if place in kept or place - 1 in kept:
            found.setdefault(place // per_piece, []).append(place)
    return found


def gather_kernel(nb, per_piece, kept, count, extra, *refs):
    found = places_in(kept, nb, per_piece)
    in_refs, out_refs = refs[: len(refs) - len(found) - extra], refs[-len(found) :]
    tail = len(kept) * count
    block = in_refs[0].shape[-1]
    sources = []
    for ref in in_refs:
        for index in range(ref.shape[0]):
            sources.append(ref.at[index])
    for out_ref, (apart, places) in zip(out_refs, found.items()):
        for part, place in enumerate(places):
            sums = [jnp.zeros((count, block), jnp.float32) for _ in range(ANC_DEV)]
            for source in sources:
                empty = source[pl.ds(tail, 1), :]
                slot = source[pl.ds(tail + 1 + apart, 1), :]
                value = jnp.zeros((count, block), jnp.float32)
                if place in kept:
                    value = jnp.where(empty > place, source[pl.ds(kept.index(place) * count, count), :], value)
                if place - 1 in kept:
                    value = jnp.where(empty < place, source[pl.ds(kept.index(place - 1) * count, count), :], value)
                for index in range(ANC_DEV):
                    sums[index] += jnp.where(slot == index, value, 0.0)
            for index in range(ANC_DEV):
                out_ref[index, part] = sums[index]


def pick_kernel(first, in_ref, *refs):
    refs[-1][...] = in_ref[first:]


def pick(params, blocks, first, earlier):
    return pl.pallas_call(
        functools.partial(pick_kernel, first),
        out_shape=jax.ShapeDtypeStruct((blocks.shape[0] - first, *blocks.shape[1:]), blocks.dtype),
        in_specs=[vmem_spec()] + [pl.BlockSpec(memory_space=pl.ANY)] * len(earlier),
        out_specs=vmem_spec(),
        compiler_params=params,
    )(blocks, *earlier)


def pack_kernel(chip, same_ref, crossed_ref, *refs):
    refs[-1][0] = same_ref[chip]
    refs[-1][1] = crossed_ref[chip]


def pack(params, chip, same, crossed, *earlier):
    return pl.pallas_call(
        functools.partial(pack_kernel, chip),
        out_shape=jax.ShapeDtypeStruct((2, *same.shape[1:]), jnp.float32),
        in_specs=[vmem_spec()] * 2 + [pl.BlockSpec(memory_space=pl.ANY)] * len(earlier),
        out_specs=vmem_spec(),
        compiler_params=params,
    )(same, crossed, *earlier)


def gather(params, nb, per_piece, kept, arrived, earlier):
    block = arrived[0].shape[-1]
    count = (arrived[0].shape[1] - META) // len(kept)
    found = places_in(kept, nb, per_piece)
    return pl.pallas_call(
        functools.partial(gather_kernel, nb, per_piece, kept, count, len(earlier)),
        out_shape=[jax.ShapeDtypeStruct((ANC_DEV, len(places), count, block), jnp.float32) for places in found.values()],
        in_specs=[vmem_spec()] * len(arrived) + [pl.BlockSpec(memory_space=pl.ANY)] * len(earlier),
        out_specs=[vmem_spec()] * len(found),
        compiler_params=params,
        cost_estimate=pl.CostEstimate(flops=0, bytes_accessed=GATHER_COST, transcendentals=0),
    )(*arrived, *earlier)


def add_kernel(places, *refs):
    came_ref, out_refs = refs[len(places)], refs[-len(places) :]
    for held_ref, place, out_ref in zip(refs, places, out_refs):
        out_ref[...] = held_ref[...] + came_ref[place]


def send(held, apart):
    going = [index for index in held if index & apart]
    return going, swapped(jnp.stack([held[index] for index in going]), "subtree", apart)


def settle(params, held, parts, apart, going, came, earlier):
    parts.append(came[going.index(apart)])
    for index in going:
        del held[index]
    kept = [index ^ apart for index in going if index != apart]
    if kept:
        sums = pl.pallas_call(
            functools.partial(add_kernel, [going.index(index ^ apart) for index in kept]),
            out_shape=[jax.ShapeDtypeStruct(came.shape[1:], came.dtype)] * len(kept),
            in_specs=[vmem_spec()] * (len(kept) + 1) + [pl.BlockSpec(memory_space=pl.ANY)] * len(earlier),
            out_specs=[vmem_spec()] * len(kept),
            compiler_params=params,
        )(*[held[index] for index in kept], came, *earlier)
        held.update(zip(kept, sums))


def finish_kernel(chunk_rows, shares, near_ref, *refs):
    out_ref = refs[-1]
    start = at = 0
    for count, share in zip(chunk_rows, shares):
        rows = pl.ds(start, count)
        for part in range(out_ref.shape[2]):
            total = refs[at + 1][:, part]
            for came in refs[at + 2 : at + share]:
                total += came[:, part]
            if part < near_ref.shape[1]:
                total += near_ref[:, part, rows]
            if part > 0:
                total += refs[at][:, part - 1]
            out_ref[0, :, part, rows, :] = total
        start += count
        at += share


def per_device_blocks(panels, pattern, child_map, ancestor_map):
    row_total, pivot_width = panels.shape[2:]
    nb = child_map.shape[2]
    block = row_total // nb
    subs = lax.axis_size("subtree")
    trees = lax.axis_size("forest")
    per_piece = nb // subs
    units = block // CUT
    chunk_rows = []
    for index, share in enumerate(CHUNK_PARTS):
        chunk_rows.append(units * share // sum(CHUNK_PARTS) * CUT)
    chunk_rows[-1] += block - sum(chunk_rows)
    chips = trees // 2
    params = pltpu.CompilerParams(vmem_limit_bytes=VMEM_LIMIT)

    panel = panels.reshape(row_total, pivot_width)
    spans = []
    for count in chunk_rows:
        spans.append((sum(chunk_rows[: len(spans)]), count))
    slots = [swapped(ancestor_map, "subtree", apart) for apart in range(1, subs)]
    updates = pl.pallas_call(
        functools.partial(multiply_kernel, nb, per_piece, spans),
        out_shape=[jax.ShapeDtypeStruct((nb, nb * count, block), jnp.float32) for count in chunk_rows]
        + [jax.ShapeDtypeStruct((2, nb), jnp.int32)],
        in_specs=[pl.BlockSpec(memory_space=pltpu.HBM)] * 4,
        out_specs=[vmem_spec()] * len(spans) + [smem_spec()],
        scratch_shapes=[
            pltpu.VMEM((row_total, pivot_width), jnp.bfloat16),
            pltpu.SMEM(child_map.shape, jnp.int32),
            pltpu.SMEM(pattern.shape, jnp.int32),
            pltpu.SMEM(ancestor_map.shape, jnp.int32),
            pltpu.SemaphoreType.DMA((nb + 3,)),
        ],
        compiler_params=params,
        cost_estimate=pl.CostEstimate(
            flops=2 * nb * block * row_total * pivot_width,
            bytes_accessed=2 * row_total * pivot_width,
            transcendentals=0,
        ),
    )(*[pltpu.with_memory_space_constraint(array, pltpu.HBM) for array in (child_map, pattern, ancestor_map, panel)])
    plan = updates[-1]
    far = list(range(1, nb - 1))
    shipments = [(far, [chunk]) for chunk in range(len(chunk_rows))]
    shipments.append(([0], list(range(len(chunk_rows)))))
    laid = []
    earlier = []
    for group in (shipments[:1], shipments[1:]):
        used = chunk_rows[:1] if not laid else chunk_rows
        rows = [shipment_rows(shipment, chunk_rows) for shipment in group]
        blocks = pl.pallas_call(
            functools.partial(route_kernel, nb, per_piece, subs, group, used, len(earlier)),
            out_shape=jax.ShapeDtypeStruct((trees, sum(rows), block), jnp.float32),
            in_specs=[smem_spec()] * subs
            + [vmem_spec()] * len(used)
            + [pl.BlockSpec(memory_space=pl.ANY)] * len(earlier),
            out_specs=vmem_spec(),
            scratch_shapes=[pltpu.SMEM((subs, nb), jnp.int32)],
            compiler_params=params,
        )(plan, *slots, *updates[: len(used)], *earlier)
        other = blocks[chips:] if not laid else pick(params, blocks, chips, going_out)
        same, crossed = blocks[:chips], swapped(other, "forest", 1)
        at = 0
        for count in rows:
            laid.append((same[:, at : at + count], crossed[:, at : at + count]))
            at += count
        if not earlier:
            going_out = [pack(params, chip, *laid[0]) for chip in range(1, chips)]
            earlier = [blocks]

    pieces = []
    open_sums = None
    for c, (kept, _) in enumerate(shipments):
        arrived = [laid[c][0][:1], laid[c][1][:1]]
        for chip in range(1, chips):
            arrived.append(swapped(going_out[chip - 1], "forest", 2 * chip))
        last = c == len(shipments) - 1
        queued = []
        waits = []
        for chip in range(1, chips):
            if open_sums is not None and chip == chips - 1:
                held, apart = open_sums[0], 1
                settle(params, held, pieces[-1], apart, *open_sums[1:], waits)
                waits = waits + list(held.values())[1:]
                while 2 * apart < subs:
                    apart *= 2
                    settle(params, held, pieces[-1], apart, *send(held, apart), [])
            if not last:
                earlier = [arrived[index + 1] for index in DEPS[chip - 1]]
                if chip == 2 and c > 1 and ZDEP:
                    earlier.append(pieces[c - 2][-1])
                if chip == chips - 1:
                    earlier += waits[chip - 1 :]
                queued.append(pack(params, chip, *laid[c + 1], *earlier))
                waits = waits[: chip - 1] + queued[-1:] + waits[chip - 1 :]
        going_out = queued
        sums = gather(params, nb, per_piece, kept, arrived, waits)
        if last:
            near = sums[0]
            break
        parts = [sums[0]]
        open_sums = None
        if c == len(chunk_rows) - 1 and DIRECT:
            for apart in range(1, subs):
                parts.append(swapped(sums[apart], "subtree", apart))
        else:
            held = dict(enumerate(sums))
            open_sums = (held, *send(held, 1))
        pieces.append(parts)
    out = pl.pallas_call(
        functools.partial(finish_kernel, chunk_rows, [len(parts) for parts in pieces]),
        out_shape=jax.ShapeDtypeStruct((1, ANC_DEV, per_piece, block, block), jnp.float32),
        in_specs=[vmem_spec()] * (1 + sum(len(parts) for parts in pieces)),
        out_specs=vmem_spec(),
        compiler_params=params,
    )(near, *[part for parts in pieces for part in parts])
    return out.reshape(1, ANC_DEV, per_piece * block, block)


def per_device_halving(panels, pattern, child_map, ancestor_map):
    row_total = panels.shape[2]
    pivot_width = panels.shape[3]
    block_count = child_map.shape[2]
    block_rows = row_total // block_count
    blocks = panels[0, 0].reshape(block_count, block_rows, pivot_width)
    one_hot = child_map[0, 0][:, None] == jnp.arange(block_count, dtype=jnp.int32)[None, :]
    reordered = jnp.einsum(
        "im,ipk->mpk", one_hot.astype(jnp.bfloat16), blocks, preferred_element_type=jnp.float32
    ).astype(jnp.bfloat16)
    flat_rows = reordered.reshape(row_total, pivot_width)
    hot_float = one_hot.astype(jnp.float32)
    moved_pattern = jnp.dot(
        jnp.dot(hot_float.T, pattern[0, 0].astype(jnp.float32), precision=lax.Precision.HIGHEST),
        hot_float,
        precision=lax.Precision.HIGHEST,
    )
    update = lax.dot_general(
        flat_rows, flat_rows, (((1,), (1,)), ((), ())), preferred_element_type=jnp.float32
    )
    update = (
        update.reshape(block_count, block_rows, block_count, block_rows)
        * moved_pattern[:, None, :, None]
    ).reshape(row_total, row_total)
    sub_count = lax.axis_size("subtree")
    depth = sub_count.bit_length() - 1
    my_index = lax.axis_index("subtree")
    holding = update
    for depth_step in range(depth):
        bit_number = depth - 1 - depth_step
        half_rows = holding.shape[0] // 2
        low_half = holding[:half_rows]
        high_half = holding[half_rows:]
        high_side = my_index >> bit_number & 1 == 1
        kept_half = jnp.where(high_side, high_half, low_half)
        sent_half = jnp.where(high_side, low_half, high_half)
        holding = kept_half + swapped(sent_half, "subtree", 1 << bit_number)
    piece_rows = holding.shape[0]
    column_blocks = holding.reshape(piece_rows, block_count, block_rows).transpose(1, 0, 2)
    slot_values = ancestor_map[0, 0]
    tree_count = lax.axis_size("forest")
    every_slot = lax.all_gather(slot_values, "forest", axis=0, tiled=True)
    owner_of = slot_values // ANC_DEV
    owner_hot = (owner_of[:, None] == jnp.arange(tree_count, dtype=jnp.int32)[None, :]).astype(
        jnp.float32
    )
    outgoing = jnp.einsum("co,cpq->opq", owner_hot, column_blocks, precision=lax.Precision.HIGHEST)
    incoming = lax.all_to_all(outgoing, "forest", split_axis=0, concat_axis=0, tiled=True)
    forest_index = lax.axis_index("forest")
    every_slot = every_slot.reshape(tree_count, block_count)
    mine_mask = every_slot // ANC_DEV == forest_index
    local_slot = every_slot % ANC_DEV
    source_hot = jnp.sum(
        jnp.where(
            mine_mask[:, :, None],
            (local_slot[:, :, None] == jnp.arange(ANC_DEV, dtype=jnp.int32)[None, None, :]).astype(
                jnp.float32
            ),
            0.0,
        ),
        axis=1,
    )
    summed = jnp.einsum("sk,spq->kpq", source_hot, incoming, precision=lax.Precision.HIGHEST)
    return summed[None]


def solution(mesh):
    in_specs = (
        P("subtree", "forest", None, None),
        P("subtree", "forest", None, None),
        P("subtree", "forest", None),
        P("subtree", "forest", None),
    )
    out_specs = P("subtree", "forest", None, None)

    def per_device(panels, pattern, child_map, ancestor_map):
        nb = child_map.shape[2]
        subs, trees = mesh.shape["subtree"], mesh.shape["forest"]
        if nb == trees and nb % (2 * subs) == 0 and subs < META and trees <= 4096:
            return per_device_blocks(panels, pattern, child_map, ancestor_map)
        return per_device_halving(panels, pattern, child_map, ancestor_map)

    return jax.shard_map(
        per_device, mesh=mesh, in_specs=in_specs, out_specs=out_specs, check_vma=False
    )
```
